128 devices in a mesh: seq: 64 (over y, z, x_hi, core), head: 2 (over x_lo).
Axes of the slice: x: 4 (x_hi: 2, x_lo: 2; x = x_hi * 2 + x_lo), y: 4, z: 4, core: 2. Of those that a mesh axis runs over, the one named last changes fastest.
Arguments:
- activations: bfloat16 [512, 256, 768], P('seq'), may hold values from -13 to 13
- w_query: bfloat16 [768, 768], P(None, 'head'), may hold values from -0.21875 to 0.21875
- w_key: bfloat16 [768, 768], P(None, 'head'), may hold values from -0.21875 to 0.21875
- w_value: bfloat16 [768, 768], P(None, 'head'), may hold values from -0.21875 to 0.21875
- w_out: bfloat16 [768, 768], P('head'), may hold values from -0.21875 to 0.21875
- cotangent: bfloat16 [512, 256, 768], P('seq'), may hold values from -6 to 6
Outputs:
- output: bfloat16 [512, 256, 768], P('seq', None, 'head')
- input_grad: bfloat16 [512, 256, 768], P('seq', None, 'head')
The draws below stay inside these ranges and needn't reach their ends.
All inputs are finite; a program needn't handle non-finite values.
Results may differ from the reference program's by a relative error of at most 0.013.
Values may be sent and summed in bfloat16 or wider, within the bound.
A program may use at most 128 MiB of HBM per device.

```python
import math
import jax
import jax.numpy as jnp
from jax import lax

D = 768
HEADS = 12
HEAD_DIM = 64
RESIDUES = 256
SEQS = 512
HD = 768


def draw_activations(key, part):
    key = jax.random.fold_in(key, 11)
    first = jax.random.fold_in(key, 0)
    values = jnp.clip(jax.random.normal(first, (SEQS, RESIDUES, D), jnp.float32), -6.0, 6.0)
    return values.astype(jnp.bfloat16)


def shard_levels(own_key, dims, cuts, smallest, largest):
    factor_of, own = 1.0, jax.random.fold_in(own_key, 6)
    for dim, blocks in cuts:
        draws = jnp.exp(jax.random.uniform(jax.random.fold_in(own, dim), (blocks,), jnp.float32, smallest / len(cuts), largest / len(cuts)))
        factor_of = factor_of * jnp.repeat(draws, dims[dim] // blocks).reshape([-1 if axis == dim else 1 for axis in range(len(dims))])
    return factor_of


def scatter_about(rng, dims, width, limit, cuts=(), held_as=jnp.bfloat16):
    drawn = jax.random.normal(rng, dims, jnp.float32) * width
    if len(cuts) > 0:
        drawn = shard_levels(rng, dims, cuts, -0.22, 0.18) * drawn
    return jnp.clip(drawn, min=-limit, max=limit).astype(held_as)


def setup_inputs(seed: int = 0) -> dict:
    streams_of = jax.random.split(jax.random.key(seed), 7)
    return {
        "activations": draw_activations(jax.random.fold_in(streams_of[6], 71), 0),
        "w_query": scatter_about(streams_of[1], (D, HD), D ** -0.5, 0.21875, ((1, 2),)),
        "w_key": scatter_about(streams_of[2], (D, HD), D ** -0.5, 0.21875, ((1, 2),)),
        "w_value": scatter_about(streams_of[3], (D, HD), D ** -0.5, 0.21875, ((1, 2),)),
        "w_out": scatter_about(streams_of[4], (HD, D), HD ** -0.5, 0.21875, ((0, 2),)),
        "cotangent": scatter_about(streams_of[5], (SEQS, RESIDUES, D), 1.0, 6.0, ((0, 64),)),
    }


def reference(activations, w_query, w_key, w_value, w_out, cotangent):
    flat = activations.reshape(-1, D)
    shape = (SEQS, RESIDUES, HEADS, HEAD_DIM)
    query = jnp.dot(flat, w_query, preferred_element_type=jnp.float32).astype(jnp.bfloat16).reshape(shape)
    keys = jnp.dot(flat, w_key, preferred_element_type=jnp.float32).astype(jnp.bfloat16).reshape(shape)
    values = jnp.dot(flat, w_value, preferred_element_type=jnp.float32).astype(jnp.bfloat16).reshape(shape)
    scale = 1.0 / (math.sqrt(HEAD_DIM) * math.sqrt(SEQS))
    logits = jnp.einsum('sihc,sjhc->hij', query.astype(jnp.float32), keys.astype(jnp.float32)) * scale
    top = lax.optimization_barrier(jnp.max(logits, axis=-1, keepdims=True))
    expd = jnp.exp(logits - top)
    probs = (expd / lax.optimization_barrier(jnp.sum(expd, axis=-1, keepdims=True))).astype(jnp.bfloat16)
    pfloat = probs.astype(jnp.float32)
    attended = jnp.einsum('hij,sjhc->sihc', pfloat, values.astype(jnp.float32)).astype(jnp.bfloat16)
    output = jnp.dot(attended.reshape(-1, HD), w_out, preferred_element_type=jnp.float32)
    output = output.astype(jnp.bfloat16).reshape(SEQS, RESIDUES, D)
    grad_attended = jnp.dot(cotangent.reshape(-1, D), w_out.T, preferred_element_type=jnp.float32)
    grad_attended = grad_attended.astype(jnp.bfloat16).reshape(shape).astype(jnp.float32)
    dprob = jnp.einsum('sihc,sjhc->hij', grad_attended, values.astype(jnp.float32))
    grad_logits = (pfloat * (dprob - lax.optimization_barrier(jnp.sum(pfloat * dprob, axis=-1, keepdims=True))) * scale).astype(jnp.bfloat16)
    glf = grad_logits.astype(jnp.float32)
    grad_query = jnp.einsum('hij,sjhc->sihc', glf, keys.astype(jnp.float32)).astype(jnp.bfloat16)
    grad_key = jnp.einsum('hij,sihc->sjhc', glf, query.astype(jnp.float32)).astype(jnp.bfloat16)
    grad_value = jnp.einsum('hij,sihc->sjhc', pfloat, grad_attended).astype(jnp.bfloat16)
    total = jnp.dot(grad_query.reshape(-1, HD), w_query.T, preferred_element_type=jnp.float32)
    total = total + jnp.dot(grad_key.reshape(-1, HD), w_key.T, preferred_element_type=jnp.float32)
    total = total + jnp.dot(grad_value.reshape(-1, HD), w_value.T, preferred_element_type=jnp.float32)
    input_grad = total.astype(jnp.bfloat16).reshape(SEQS, RESIDUES, D)
    return (output, input_grad)
```

```python
import functools
import math

import jax
import jax.numpy as jnp
from jax import lax
from jax.experimental import pallas as pl
from jax.experimental.pallas import tpu as pltpu
from jax.sharding import PartitionSpec as P

MESH = pl.DeviceIdType.MESH
BF, F32 = jnp.bfloat16, jnp.float32
S, R, D, HW, HD = 8, 256, 768, 384, 64
NT = (((1,), (1,)), ((), ()))
NN = (((1,), (0,)), ((), ()))
OWN = (0, 384, 768)
OTH = (1920, 1536, 1152)


def dot(a, b, dims=NN):
    return lax.dot_general(a, b, dims, preferred_element_type=F32)


def low_half(shape):
    return lax.broadcasted_iota(jnp.int32, shape, 1) < HD


def kernel(scale, act_hbm, wq_hbm, wk_hbm, wv_hbm, wo_hbm, cot_hbm, out_hbm, ig_hbm,
           act, cot, wn, ws, won, wos, xf, g2a, g2b, igp, keep, xs, xr, rsend, rrecv, pbuf, gat, outv, igv,
           load_sem, w_ss, w_rs, wc_ss, wc_rs, xc_ss, xc_rs, rs_ss, rs_rs, p_ss, p_rs,
           a1_ss, a1_rs, a2_ss, a2_rs, gc_ss, gc_rs, o_sem):
    seq, h = lax.axis_index("seq"), lax.axis_index("head")
    c, xh, z, y = seq % 2, (seq // 2) % 2, (seq // 4) % 4, seq // 16
    x = xh * 2 + h

    def dev(yy, zz, xx, cc):
        return (((yy % 4) * 4 + zz % 4) * 2 + (xx % 4) // 2) * 2 + cc, xx % 2

    sibling = dev(y, z, x, 1 - c)

    def remote(src, dst, ss, rs, to):
        return pltpu.make_async_remote_copy(
            src_ref=src, dst_ref=dst, send_sem=ss, recv_sem=rs, device_id=to, device_id_type=MESH)

    loads = [
        pltpu.make_async_copy(wq_hbm, wn.at[:, 0:384], load_sem.at[16]),
        pltpu.make_async_copy(wk_hbm, wn.at[:, 384:768], load_sem.at[17]),
        pltpu.make_async_copy(wv_hbm, wn.at[:, 768:1152], load_sem.at[18]),
        pltpu.make_async_copy(wo_hbm, won.at[0:384], load_sem.at[19]),
    ]

    def load_seq(hbm, buf, s, sem):
        return pltpu.make_async_copy(hbm.at[s], buf.at[s], load_sem.at[sem])

    loads[0].start()
    loads[1].start()
    for t in range(4):
        load_seq(act_hbm, act, t, t).start()
        load_seq(act_hbm, act, t + 4, t + 4).start()
    loads[2].start()
    loads[3].start()
    for s in range(S):
        load_seq(cot_hbm, cot, s, 8 + s).start()

    bar = pltpu.get_barrier_semaphore()

    def greet(to):
        pl.semaphore_signal(bar, inc=1, device_id=to, device_id_type=MESH)

    greet(sibling)

    def greet_rs(d, _):
        greet(dev(y + d // 8, z + (d // 2) % 4, x + 2 * (d % 2), c))
        return 0

    lax.fori_loop(1, 32, greet_rs, 0)

    def greet_odd(d, _):
        greet(dev(y, z + d // 2, x + 1 + 2 * (d % 2), c))
        return 0

    lax.fori_loop(0, 8, greet_odd, 0)

    def greet_odd_y(d, _):
        greet(dev(y + d // 2, z, x + 1 + 2 * (d % 2), c))
        return 0

    lax.fori_loop(2, 8, greet_odd_y, 0)

    def swap_lanes(first, count):
        def rows(r, _):
            at = pl.ds(r * 128, 128)
            for j in range(first, first + count):
                block = wn[at, 128 * j:128 * j + 128]
                ws[at, 128 * j:128 * j + 128] = jnp.concatenate([block[:, HD:], block[:, :HD]], axis=1)
            return 0
        lax.fori_loop(0, 6, rows, 0)

    def swap_rows(base):
        for g in range(3):
            at = base + 128 * g
            wos[at:at + 64, :] = won[at + 64:at + 128, :]
            wos[at + 64:at + 128, :] = won[at:at + 64, :]

    def put(kind, head, t, even, odd):
        low = low_half(even.shape)
        lanes = pl.ds(pl.multiple_of(t * 128, 128), 128)
        xf[kind, head, :, lanes] = jnp.where(low, even, odd)
        xf[kind, head + 1, :, lanes] = jnp.where(low, odd, even)

    def project(t, lanes, places):
        even = dot(act[t], wn[:, lanes[0]:lanes[1]]).astype(BF)
        odd = dot(act[t + 4], ws[:, lanes[0]:lanes[1]]).astype(BF)
        for j, (kind, head) in enumerate(places):
            put(kind, head, t, even[:, 128 * j:128 * j + 128], odd[:, 128 * j:128 * j + 128])

    def project_ga(t, half):
        even = dot(cot[t], won[384 * half:384 * half + 384, :], NT).astype(BF)
        odd = dot(cot[t + 4], wos[384 * half:384 * half + 384, :], NT).astype(BF)
        for g in range(3):
            put(3, 6 * half + 2 * g, t, even[:, 128 * g:128 * g + 128], odd[:, 128 * g:128 * g + 128])

    loads[0].wait()
    loads[1].wait()
    swap_lanes(0, 6)

    def own_qk(t, _):
        load_seq(act_hbm, act, t, t).wait()
        load_seq(act_hbm, act, t + 4, t + 4).wait()
        project(t, (0, 768), [(0, 0), (0, 2), (0, 4), (1, 0), (1, 2), (1, 4)])
        return 0

    lax.fori_loop(0, 4, own_qk, 0)

    pl.semaphore_wait(bar, 46)

    def weight_copies():
        out = []
        for way, to in ((0, dev(y, z, x + 1, c)), (1, dev(y, z, x + 3, c))):
            rows = pl.ds(pl.multiple_of((2 * c + way) * 192, 192), 192)
            for i, src in enumerate((wq_hbm, wk_hbm, wv_hbm)):
                out.append(remote(src.at[rows], wn.at[rows, OTH[i]:OTH[i] + 384], w_ss.at[way, i], w_rs.at[way, i], to))
            rows = pl.ds(pl.multiple_of((2 * c + way) * 96, 96), 96)
            dst = pl.ds(pl.multiple_of(384 + (2 * c + way) * 96, 96), 96)
            out.append(remote(wo_hbm.at[rows], won.at[dst], w_ss.at[way, 3], w_rs.at[way, 3], to))
        return out

    def weight_forwards():
        out = []
        rows = pl.ds(pl.multiple_of(c * 384, 384), 384)
        for i in range(3):
            ref = wn.at[rows, OTH[i]:OTH[i] + 384]
            out.append(remote(ref, ref, wc_ss.at[i], wc_rs.at[i], sibling))
        ref = won.at[pl.ds(pl.multiple_of(384 + c * 192, 192), 192)]
        out.append(remote(ref, ref, wc_ss.at[3], wc_rs.at[3], sibling))
        return out

    for copy in weight_copies():
        copy.start()

    def pair_sum(left, right, owner):
        def head(i, _):
            total = dot(xf[left, i], xf[right, i], NT)

            @pl.when(c == owner)
            def _():
                keep[pl.ds(pl.multiple_of(i * 256, 256), 256), :] = total

            @pl.when(c != owner)
            def _():
                xs[pl.ds(pl.multiple_of(i * 256, 256), 256), :] = total.astype(BF)
            return 0
        lax.fori_loop(0, 6, head, 0)

    core_copy = remote(xs, xr, xc_ss, xc_rs, sibling)

    pair_sum(0, 1, 0)

    @pl.when(c == 1)
    def _():
        core_copy.start()

    loads[2].wait()
    swap_lanes(6, 3)
    loads[3].wait()
    swap_rows(0)

    def own_v(t, _):
        project(t, (768, 1152), [(2, 0), (2, 2), (2, 4)])
        return 0

    lax.fori_loop(0, 4, own_v, 0)

    me = (y * 4 + z) * 2 + xh

    def rs_copy(d):
        yy, zz, hh = (y + d // 8) % 4, (z + (d // 2) % 4) % 4, (xh + d % 2) % 2
        n = (yy * 4 + zz) * 2 + hh
        return remote(rsend.at[:, n], rrecv.at[d], rs_ss.at[d], rs_rs.at[d], dev(yy, zz, hh * 2 + h, c))

    def send_sums():
        core_copy.wait_recv()

        def add(i, _):
            at = pl.ds(pl.multiple_of(i * 256, 256), 256)
            total = (keep[at, :] + xr[at, :].astype(F32)).astype(BF)
            rsend[i // 2, pl.ds((i % 2) * 16, 16)] = total.reshape(16, 16, 256)
            return 0

        lax.fori_loop(0, 6, add, 0)

        def start(d, _):
            rs_copy(d).start()
            return 0

        lax.fori_loop(1, 32, start, 0)

    def take_sums():
        def wait(d, _):
            rs_copy(d).wait_recv()
            return 0

        lax.fori_loop(1, 32, wait, 0)

        def add(d, total):
            return total + rrecv[d].astype(F32)

        return lax.fori_loop(1, 32, add, rsend[:, me].astype(F32))

    def a1_copy(k, d):
        ref = gat.at[c, h, k, y, z, xh]
        u, v = d // 4, d % 4
        to = (dev(y + u, z + v, x, c), dev(y, z + u, x + v, c), dev(y + u, z, x + v, c))[k]
        return remote(ref, ref, a1_ss.at[k, d], a1_rs.at[k, d], to)

    def gather_own(block):
        for k in range(3):
            gat[c, h, k, y, z, xh] = block[k]

        def start(d, _):
            for k in range(3):
                a1_copy(k, d).start()
            return 0

        lax.fori_loop(1, 16, start, 0)

    def plane(k, yy, zz, xx):
        if k == 0:
            return gat.at[c, xx % 2, 0, :, :, xx // 2]
        if k == 1:
            return gat.at[c, :, 1, yy]
        return gat.at[c, :, 2, :, zz]

    def a2_copy(k, d):
        ref = plane(k, y, z, x)
        to = (dev(y, z, x + d, c), dev(y + d, z, x, c), dev(y, z + d, x, c))[k]
        return remote(ref, ref, a2_ss.at[k, d], a2_rs.at[k, d], to)

    def forward(k, d):
        ref = plane(k, (y + 4 - d) % 4, (z + 4 - d) % 4, (x + 4 - d) % 4)
        return remote(ref, ref, gc_ss.at[k, d], gc_rs.at[k, d], sibling)

    def gather_planes():
        for k in range(3):
            def wait(d, _):
                a1_copy(k, d).wait_recv()
                return 0

            lax.fori_loop(1, 16, wait, 0)
            for d in (2, 1, 3):
                a2_copy(k, d).start()
            forward(k, 0).start()

    def gather_rest():
        for d in (1, 3, 2):
            for k in range(3):
                a2_copy(k, d).wait_recv()
                forward(k, d).start()

    def gather_other():
        for k in range(3):
            for d in range(4):
                forward(k, d).wait_recv()

    p_copy = remote(pbuf, pbuf, p_ss, p_rs, sibling)

    def softmax_step():
        logits = take_sums() * scale
        top = jnp.max(logits, axis=-1, keepdims=True)
        expd = jnp.exp(logits - top)
        probs = (expd / jnp.sum(expd, axis=-1, keepdims=True)).astype(BF)
        pbuf[...] = probs
        p_copy.start()
        gather_own(probs)

    def grad_step():
        dprob = take_sums()
        p_copy.wait_recv()
        probs = pbuf[...].astype(F32)
        inner = jnp.sum(probs * dprob, axis=-1, keepdims=True)
        gather_own((probs * (dprob - inner) * scale).astype(BF))

    def on_core(core, step):
        pl.when(c == core)(step)

    on_core(0, send_sums)

    def own_ga(t, _):
        load_seq(cot_hbm, cot, t, 8 + t).wait()
        load_seq(cot_hbm, cot, t + 4, 12 + t).wait()
        project_ga(t, 0)
        return 0

    lax.fori_loop(0, 4, own_ga, 0)
    pair_sum(3, 2, 1)
    on_core(0, core_copy.start)
    on_core(1, send_sums)

    for copy in weight_copies():
        copy.wait_recv()
    for copy in weight_forwards():
        copy.start()
    on_core(0, softmax_step)
    for copy in weight_forwards():
        copy.wait_recv()
    swap_lanes(9, 9)
    swap_rows(384)

    def other_qkv(t, _):
        project(t, (1152, 2304),
                [(2, 6), (2, 8), (2, 10), (1, 6), (1, 8), (1, 10), (0, 6), (0, 8), (0, 10)])
        return 0

    def other_ga(t, _):
        project_ga(t, 1)
        return 0

    lax.fori_loop(0, 2, other_qkv, 0)
    on_core(1, grad_step)
    on_core(0, gather_planes)
    lax.fori_loop(2, 4, other_qkv, 0)
    lax.fori_loop(0, 4, other_ga, 0)
    on_core(1, gather_planes)
    on_core(0, gather_rest)
    on_core(1, gather_other)

    def pair_of(arr, g):
        half = (h + g // 3) % 2
        block = gat[arr, half, g % 3].reshape(512, 256)
        return block[:256], block[256:]

    def unput(first, second, refs):
        first, second = first.astype(BF), second.astype(BF)
        low = low_half((256, 128))
        for t in range(4):
            one, two = first[:, 128 * t:128 * t + 128], second[:, 128 * t:128 * t + 128]
            ref, lanes = refs
            ref[t, :, lanes] = jnp.where(low, one, two)
            ref[t + 4, :, lanes] = jnp.where(low, two, one)

    def lanes_at(start):
        return pl.ds(pl.multiple_of(start, 128), 128)

    att, gv = act, cot

    def with_probs(g, _):
        p0, p1 = pair_of(0, g)
        at = lanes_at(128 * g)
        unput(dot(p0, xf[2, 2 * g]), dot(p1, xf[2, 2 * g + 1]), (att, at))
        unput(dot(p0.T, xf[3, 2 * g]), dot(p1.T, xf[3, 2 * g + 1]), (gv, at))
        return 0

    lax.fori_loop(0, 6, with_probs, 0)

    own_cols = pl.ds(pl.multiple_of(h * 384, 384), 384)

    def out_copy(s):
        return pltpu.make_async_copy(outv.at[s], out_hbm.at[s], o_sem.at[s])

    def ig_copy(s):
        return pltpu.make_async_copy(igv.at[s], ig_hbm.at[s], o_sem.at[8 + s])

    def from_probs(t, _):
        for s, w_o, w in ((t, won, wn), (t + 4, wos, ws)):
            outv[s] = dot(att[s], w_o[:, own_cols]).astype(BF)
            out_copy(s).start()
            igp[s] = dot(gv[s], w[own_cols, 768:1536], NT)
        return 0

    lax.fori_loop(0, 4, from_probs, 0)
    on_core(1, gather_rest)
    on_core(0, gather_other)

    def with_grads(g, _):
        l0, l1 = pair_of(1, g)
        gq0, gq1 = dot(l0, xf[1, 2 * g]), dot(l1, xf[1, 2 * g + 1])
        gk0, gk1 = dot(l0.T, xf[0, 2 * g]), dot(l1.T, xf[0, 2 * g + 1])

        @pl.when(g < 3)
        def _():
            unput(gq0, gq1, (g2a, lanes_at(128 * g)))
            unput(gk0, gk1, (g2a, lanes_at(384 + 128 * g)))

        @pl.when(g >= 3)
        def _():
            unput(gk0, gk1, (g2b, lanes_at(128 * (g - 3))))
            unput(gq0, gq1, (g2b, lanes_at(384 + 128 * (g - 3))))
        return 0

    lax.fori_loop(0, 6, with_grads, 0)

    def from_grads(t, _):
        for s, w in ((t, wn), (t + 4, ws)):
            total = igp[s] + dot(g2a[s], w[own_cols, 0:768], NT) + dot(g2b[s], w[own_cols, 1536:2304], NT)
            igv[s] = total.astype(BF)
            ig_copy(s).start()
        return 0

    lax.fori_loop(0, 4, from_grads, 0)

    for copy in weight_copies() + weight_forwards():
        copy.wait_send()
    core_copy.wait_send()
    on_core(0, p_copy.wait_send)

    def rs_left(d, _):
        rs_copy(d).wait_send()
        return 0

    lax.fori_loop(1, 32, rs_left, 0)

    def a1_left(d, _):
        for k in range(3):
            a1_copy(k, d).wait_send()
        return 0

    lax.fori_loop(1, 16, a1_left, 0)
    for k in range(3):
        for d in range(4):
            if d:
                a2_copy(k, d).wait_send()
            forward(k, d).wait_send()

    def out_left(s, _):
        out_copy(s).wait()
        ig_copy(s).wait()
        return 0

    lax.fori_loop(0, S, out_left, 0)


def on_device(total_seqs, activations, w_query, w_key, w_value, w_out, cotangent):
    scale = 1.0 / (math.sqrt(HD) * math.sqrt(total_seqs))
    hbm = pl.BlockSpec(memory_space=pl.ANY)
    dma = pltpu.SemaphoreType.DMA
    result = jax.ShapeDtypeStruct((S, R, HW), BF)
    return pl.pallas_call(
        functools.partial(kernel, scale),
        out_shape=(result, result),
        in_specs=[hbm] * 6,
        out_specs=(hbm, hbm),
        scratch_shapes=[
            pltpu.VMEM((S, R, D), BF),
            pltpu.VMEM((S, R, D), BF),
            pltpu.VMEM((D, 6 * HW), BF),
            pltpu.VMEM((D, 6 * HW), BF),
            pltpu.VMEM((D, D), BF),
            pltpu.VMEM((D, D), BF),
            pltpu.VMEM((4, 12, R, 512), BF),
            pltpu.VMEM((S, R, D), BF),
            pltpu.VMEM((S, R, D), BF),
            pltpu.VMEM((S, R, HW), F32),
            pltpu.VMEM((6 * R, R), F32),
            pltpu.VMEM((6 * R, R), BF),
            pltpu.VMEM((6 * R, R), BF),
            pltpu.VMEM((3, 32, 16, R), BF),
            pltpu.VMEM((32, 3, 16, R), BF),
            pltpu.VMEM((3, 16, R), BF),
            pltpu.VMEM((2, 2, 3, 4, 4, 2, 16, R), BF),
            pltpu.VMEM((S, R, HW), BF),
            pltpu.VMEM((S, R, HW), BF),
            dma((20,)),
            dma((2, 4)), dma((2, 4)), dma((4,)), dma((4,)),
            dma, dma,
            dma((32,)), dma((32,)),
            dma, dma,
            dma((3, 16)), dma((3, 16)), dma((3, 4)), dma((3, 4)), dma((3, 4)), dma((3, 4)),
            dma((16,)),
        ],
        compiler_params=pltpu.CompilerParams(
            collective_id=0, has_side_effects=True, vmem_limit_bytes=62 * 2**20),
        cost_estimate=pl.CostEstimate(flops=18_500_000_000, bytes_accessed=15_000_000, transcendentals=12288),
        name="tied_row_attention",
    )(activations, w_query, w_key, w_value, w_out, cotangent)


def solution(mesh):
    total_seqs = S * mesh.shape["seq"]
    placed = (
        P("seq", None, None),
        P(None, "head"),
        P(None, "head"),
        P(None, "head"),
        P("head", None),
        P("seq", None, None),
    )
    return jax.shard_map(
        functools.partial(on_device, total_seqs),
        mesh=mesh,
        in_specs=placed,
        out_specs=(P("seq", None, "head"), P("seq", None, "head")),
        check_vma=False,
    )
```

```python
import functools
import math

import jax
import jax.numpy as jnp
from jax import lax
from jax.experimental import pallas as pl
from jax.experimental.pallas import tpu as pltpu
from jax.sharding import PartitionSpec as P

MESH = pl.DeviceIdType.MESH
BF, F32 = jnp.bfloat16, jnp.float32
S, R, D, HW, HD = 8, 256, 768, 384, 64
NT = (((1,), (1,)), ((), ()))
NN = (((1,), (0,)), ((), ()))
OWN = (0, 384, 768)
OTH = (1920, 1536, 1152)


def dot(a, b, dims=NN):
    return lax.dot_general(a, b, dims, preferred_element_type=F32)


def low_half(shape):
    return lax.broadcasted_iota(jnp.int32, shape, 1) < HD


def kernel(scale, act_hbm, wq_hbm, wk_hbm, wv_hbm, wo_hbm, cot_hbm, out_hbm, ig_hbm,
           act, cot, wn, ws, won, wos, xf, g2a, g2b, igp, keep, xs_l, xs_d, xr, rsend, rrecv, half_send, half_recv, pbuf, gat, outv, igv,
           load_sem, w_ss, w_rs, wc_ss, wc_rs, xc_ss, xc_rs, rs_ss, rs_rs, hc_ss, hc_rs, p_ss, p_rs,
           a1_ss, a1_rs, a2_ss, a2_rs, gc_ss, gc_rs, o_sem):
    seq, h = lax.axis_index("seq"), lax.axis_index("head")
    rem, div = lax.rem, lax.div
    c, xh, z, y = rem(seq, 2), rem(div(seq, 2), 2), rem(div(seq, 4), 4), div(seq, 16)
    ys, zs = [y], [z]
    for d in (1, 2, 3):
        ys.append(rem(y + d, 4))
        zs.append(rem(z + d, 4))
    x = xh * 2 + h
    xs_of = [(xh, h)]
    for d in (1, 2, 3):
        xx = rem(x + d, 4)
        xs_of.append((div(xx, 2), rem(xx, 2)))

    def dev(dy, dz, dx, cc=c):
        return ys[dy] * 16 + zs[dz] * 4 + xs_of[dx][0] * 2 + cc, xs_of[dx][1]

    sibling = dev(0, 0, 0, 1 - c)

    def remote(src, dst, ss, rs, to):
        return pltpu.make_async_remote_copy(
            src_ref=src, dst_ref=dst, send_sem=ss, recv_sem=rs, device_id=to, device_id_type=MESH)

    loads = [
        pltpu.make_async_copy(wq_hbm, wn.at[:, 0:384], load_sem.at[16]),
        pltpu.make_async_copy(wk_hbm, wn.at[:, 384:768], load_sem.at[17]),
        pltpu.make_async_copy(wv_hbm, wn.at[:, 768:1152], load_sem.at[18]),
        pltpu.make_async_copy(wo_hbm, won.at[0:384], load_sem.at[19]),
    ]

    def load_seq(hbm, buf, s, sem):
        return pltpu.make_async_copy(hbm.at[s], buf.at[s], load_sem.at[sem])

    loads[0].start()
    loads[1].start()
    for t in range(4):
        load_seq(act_hbm, act, t, t).start()
        load_seq(act_hbm, act, t + 4, t + 4).start()
    loads[2].start()
    loads[3].start()
    for s in range(S):
        load_seq(cot_hbm, cot, s, 8 + s).start()

    bar = pltpu.get_barrier_semaphore()

    def greet(to):
        pl.semaphore_signal(bar, inc=1, device_id=to, device_id_type=MESH)

    greet(sibling)
    for dy in range(4):
        for dz in range(4):
            for dx in range(4):
                if (dy, dz, dx) != (0, 0, 0) and (dx % 2 == 0 or dy == 0 or dz == 0):
                    greet(dev(dy, dz, dx))

    pl.semaphore_wait(bar, 46)

    def weight_copies():
        out = []
        for way, to in ((0, dev(0, 0, 1)), (1, dev(0, 0, 3))):
            rows = pl.ds(pl.multiple_of((2 * c + way) * 192, 192), 192)
            for i, src in enumerate((wq_hbm, wk_hbm, wv_hbm)):
                out.append(remote(src.at[rows], wn.at[rows, OTH[i]:OTH[i] + 384], w_ss.at[way, i], w_rs.at[way, i], to))
            rows = pl.ds(pl.multiple_of((2 * c + way) * 96, 96), 96)
            dst = pl.ds(pl.multiple_of(384 + (2 * c + way) * 96, 96), 96)
            out.append(remote(wo_hbm.at[rows], won.at[dst], w_ss.at[way, 3], w_rs.at[way, 3], to))
        return out

    def weight_forwards():
        out = []
        rows = pl.ds(pl.multiple_of(c * 384, 384), 384)
        for i in range(3):
            ref = wn.at[rows, OTH[i]:OTH[i] + 384]
            out.append(remote(ref, ref, wc_ss.at[i], wc_rs.at[i], sibling))
        ref = won.at[pl.ds(pl.multiple_of(384 + c * 192, 192), 192)]
        out.append(remote(ref, ref, wc_ss.at[3], wc_rs.at[3], sibling))
        return out

    for copy in weight_copies():
        copy.start()

    def swap_lanes(first, count):
        def rows(r, _):
            at = pl.ds(r * 128, 128)
            for j in range(first, first + count):
                block = wn[at, 128 * j:128 * j + 128]
                ws[at, 128 * j:128 * j + 128] = jnp.concatenate([block[:, HD:], block[:, :HD]], axis=1)
            return 0
        lax.fori_loop(0, 6, rows, 0, unroll=True)

    def swap_rows(base):
        for g in range(3):
            at = base + 128 * g
            wos[at:at + 64, :] = won[at + 64:at + 128, :]
            wos[at + 64:at + 128, :] = won[at:at + 64, :]

    def put(kind, head, t, even, odd):
        low = low_half(even.shape)
        lanes = pl.ds(pl.multiple_of(t * 128, 128), 128)
        xf[kind, head, :, lanes] = jnp.where(low, even, odd)
        xf[kind, head + 1, :, lanes] = jnp.where(low, odd, even)

    def project(t, lanes, places):
        even = dot(act[t], wn[:, lanes[0]:lanes[1]]).astype(BF)
        odd = dot(act[t + 4], ws[:, lanes[0]:lanes[1]]).astype(BF)
        for j, (kind, head) in enumerate(places):
            put(kind, head, t, even[:, 128 * j:128 * j + 128], odd[:, 128 * j:128 * j + 128])

    def project_ga(t, half):
        even = dot(cot[t], won[384 * half:384 * half + 384, :], NT).astype(BF)
        odd = dot(cot[t + 4], wos[384 * half:384 * half + 384, :], NT).astype(BF)
        for g in range(3):
            put(3, 6 * half + 2 * g, t, even[:, 128 * g:128 * g + 128], odd[:, 128 * g:128 * g + 128])

    loads[0].wait()
    loads[1].wait()
    swap_lanes(0, 6)

    def own_qk(t, _):
        load_seq(act_hbm, act, t, t).wait()
        load_seq(act_hbm, act, t + 4, t + 4).wait()
        project(t, (0, 768), [(0, 0), (0, 2), (0, 4), (1, 0), (1, 2), (1, 4)])
        return 0

    lax.fori_loop(0, 4, own_qk, 0, unroll=True)

    def pair_sum(left, right, mine, other, first):
        def head(i, _):
            total = dot(xf[left, i], xf[right, i], NT)
            at = pl.ds(pl.multiple_of(i * 256, 256), 256)
            mine[at, :] = total
            other[at, :] = total.astype(BF)
            return 0
        lax.fori_loop(first, first + 3, head, 0, unroll=True)

    def core_copy(src, part):
        at = pl.ds(part * 768, 768)
        return remote(src.at[at], xr.at[at], xc_ss.at[part], xc_rs.at[part], sibling)

    for part in (0, 1):
        pair_sum(0, 1, keep, xs_l, 3 * part)

        @pl.when(c == 1)
        def _():
            core_copy(xs_l, part).start()

    loads[2].wait()
    swap_lanes(6, 3)
    loads[3].wait()
    swap_rows(0)

    def own_v(t, _):
        project(t, (768, 1152), [(2, 0), (2, 2), (2, 4)])
        return 0

    lax.fori_loop(0, 4, own_v, 0, unroll=True)

    me = y * 4 + z

    others = [(dy, dz) for dy in range(4) for dz in range(4)][1:]

    def rs_copy(i, dy, dz):
        return remote(rsend.at[:, ys[dy] * 4 + zs[dz]], rrecv.at[i], rs_ss, rs_rs, dev(dy, dz, 0))

    rs_all = remote(rrecv, rrecv, rs_ss, rs_rs, sibling)
    half_copy = remote(half_send, half_recv, hc_ss, hc_rs, dev(0, 0, 2))

    def send_sums():
        for part in (0, 1):
            core_copy(xs_l, part).wait_recv()

            def add(i, _):
                at = pl.ds(pl.multiple_of(i * 256, 256), 256)
                total = (keep[at, :] + xr[at, :].astype(F32)).astype(BF)
                rsend[i // 2, pl.ds((i % 2) * 8, 8)] = total.reshape(8, 2, 16, 256)
                return 0

            lax.fori_loop(3 * part, 3 * part + 3, add, 0, unroll=True)
        for i, where in enumerate(others):
            rs_copy(i, *where).start()

    def take_half(half):
        def add(d, total):
            return total + rrecv[d, :, half].astype(F32)

        return lax.fori_loop(0, 15, add, rsend[:, me, half].astype(F32), unroll=True)

    def take_sums():
        rs_all.wait_recv()
        half_send[...] = take_half(1 - xh)
        half_copy.start()
        own = take_half(xh)
        half_copy.wait_recv()
        return own + half_recv[...]

    def a1_copy(k, u, v):
        ref = gat.at[c, h, k, y, z, xh]
        to = (dev(u, v, 0), dev(0, u, v), dev(u, 0, v))[k]
        return remote(ref, ref, a1_ss.at[k], a1_rs.at[k], to)

    a1_all = [remote(rrecv.at[0:5, :, 0], rrecv.at[0:5, :, 0], a1_ss.at[k], a1_rs.at[k], sibling) for k in range(3)]

    def gather_own(block):
        for k in range(3):
            gat[c, h, k, y, z, xh] = block[k]
        for u in range(4):
            for v in range(4):
                if (u, v) != (0, 0):
                    for k in range(3):
                        a1_copy(k, u, v).start()

    def plane(k, d):
        if k == 0:
            return gat.at[c, xs_of[d][1], 0, :, :, xs_of[d][0]]
        if k == 1:
            return gat.at[c, :, 1, ys[d]]
        return gat.at[c, :, 2, :, zs[d]]

    def a2_copy(k, d):
        ref = plane(k, 0)
        to = (dev(0, 0, d), dev(d, 0, 0), dev(0, d, 0))[k]
        return remote(ref, ref, a2_ss.at[k, d], a2_rs.at[k, d], to)

    def forward(k, d):
        ref = plane(k, (4 - d) % 4)
        return remote(ref, ref, gc_ss.at[k, d], gc_rs.at[k, d], sibling)

    def gather_planes():
        for k in range(3):
            a1_all[k].wait_recv()
            for d in (2, 1, 3):
                a2_copy(k, d).start()
        for k in range(3):
            forward(k, 0).start()

    def gather_rest():
        for d in (1, 3, 2):
            for k in range(3):
                a2_copy(k, d).wait_recv()
                forward(k, d).start()

    def gather_other():
        for k in range(3):
            for d in range(4):
                forward(k, d).wait_recv()

    p_copy = remote(pbuf, pbuf, p_ss, p_rs, sibling)

    def softmax_step():
        logits = take_sums() * scale
        top = jnp.max(logits, axis=-1, keepdims=True)
        expd = jnp.exp(logits - top)
        probs = (expd / jnp.sum(expd, axis=-1, keepdims=True)).astype(BF)
        pbuf[...] = probs
        p_copy.start()
        gather_own(probs)

    def grad_step():
        dprob = take_sums()
        p_copy.wait_recv()
        probs = pbuf[...].astype(F32)
        inner = jnp.sum(probs * dprob, axis=-1, keepdims=True)
        gather_own((probs * (dprob - inner) * scale).astype(BF))

    def on_core(core, step):
        pl.when(c == core)(step)

    on_core(0, send_sums)

    def own_ga(t, _):
        load_seq(cot_hbm, cot, t, 8 + t).wait()
        load_seq(cot_hbm, cot, t + 4, 12 + t).wait()
        project_ga(t, 0)
        return 0

    lax.fori_loop(0, 4, own_ga, 0, unroll=True)
    for part in (0, 1):
        pair_sum(3, 2, keep, xs_d, 3 * part)
        on_core(0, core_copy(xs_d, part).start)
    on_core(1, send_sums)

    def other_qkv(t, _):
        project(t, (1152, 2304),
                [(2, 6), (2, 8), (2, 10), (1, 6), (1, 8), (1, 10), (0, 6), (0, 8), (0, 10)])
        return 0

    def other_ga(t, _):
        project_ga(t, 1)
        return 0

    on_core(0, softmax_step)
    for copy in weight_copies():
        copy.wait_recv()
    for copy in weight_forwards():
        copy.start()
    on_core(1, grad_step)
    for copy in weight_forwards():
        copy.wait_recv()
    swap_lanes(9, 9)
    swap_rows(384)
    lax.fori_loop(0, 2, other_qkv, 0, unroll=True)
    on_core(0, gather_planes)
    lax.fori_loop(2, 4, other_qkv, 0, unroll=True)
    lax.fori_loop(0, 4, other_ga, 0, unroll=True)
    on_core(1, gather_planes)
    on_core(0, gather_rest)
    on_core(1, gather_other)

    def pair_of(arr, g):
        half = (h + g // 3) % 2
        block = gat[arr, half, g % 3].reshape(512, 256)
        return block[:256], block[256:]

    def unput(first, second, refs):
        first, second = first.astype(BF), second.astype(BF)
        low = low_half((256, 128))
        for t in range(4):
            one, two = first[:, 128 * t:128 * t + 128], second[:, 128 * t:128 * t + 128]
            ref, lanes = refs
            ref[t, :, lanes] = jnp.where(low, one, two)
            ref[t + 4, :, lanes] = jnp.where(low, two, one)

    def lanes_at(start):
        return pl.ds(pl.multiple_of(start, 128), 128)

    att, gv = act, cot

    def with_probs(g, _):
        p0, p1 = pair_of(0, g)
        at = lanes_at(128 * g)
        unput(dot(p0, xf[2, 2 * g]), dot(p1, xf[2, 2 * g + 1]), (att, at))
        unput(dot(p0.T, xf[3, 2 * g]), dot(p1.T, xf[3, 2 * g + 1]), (gv, at))
        return 0

    lax.fori_loop(0, 6, with_probs, 0, unroll=True)

    own_cols = pl.ds(pl.multiple_of(h * 384, 384), 384)

    def out_copy(s):
        return pltpu.make_async_copy(outv.at[s], out_hbm.at[s], o_sem.at[s])

    def ig_copy(s):
        return pltpu.make_async_copy(igv.at[s], ig_hbm.at[s], o_sem.at[8 + s])

    def from_probs(t, _):
        for s, w_o, w in ((t, won, wn), (t + 4, wos, ws)):
            outv[s] = dot(att[s], w_o[:, own_cols]).astype(BF)
            out_copy(s).start()
            igp[s] = dot(gv[s], w[own_cols, 768:1536], NT)
        return 0

    lax.fori_loop(0, 2, from_probs, 0, unroll=True)
    on_core(1, gather_rest)
    lax.fori_loop(2, 4, from_probs, 0, unroll=True)
    on_core(0, gather_other)

    def with_grads(ref, first, query_at, key_at):
        def pair(i, _):
            g = first + i
            l0, l1 = pair_of(1, g)
            unput(dot(l0, xf[1, 2 * g]), dot(l1, xf[1, 2 * g + 1]), (ref, lanes_at(query_at + 128 * i)))
            unput(dot(l0.T, xf[0, 2 * g]), dot(l1.T, xf[0, 2 * g + 1]), (ref, lanes_at(key_at + 128 * i)))
            return 0
        lax.fori_loop(0, 3, pair, 0, unroll=True)

    with_grads(g2a, 0, 0, 384)
    with_grads(g2b, 3, 384, 0)

    def from_grads(t, _):
        for s, w in ((t, wn), (t + 4, ws)):
            total = igp[s] + dot(g2a[s], w[own_cols, 0:768], NT) + dot(g2b[s], w[own_cols, 1536:2304], NT)
            igv[s] = total.astype(BF)
            ig_copy(s).start()
        return 0

    for copy in weight_copies() + weight_forwards():
        copy.wait_send()
    on_core(0, p_copy.wait_send)
    rs_all.wait_send()
    half_copy.wait_send()
    for k in range(3):
        a1_all[k].wait_send()
        for d in range(4):
            if d:
                a2_copy(k, d).wait_send()
            forward(k, d).wait_send()
    for part in (0, 1):
        core_copy(xs_l, part).wait_send()

    lax.fori_loop(0, 4, from_grads, 0, unroll=True)

    def out_left(s, _):
        out_copy(s).wait()
        ig_copy(s).wait()
        return 0

    lax.fori_loop(0, S, out_left, 0)


def on_device(total_seqs, activations, w_query, w_key, w_value, w_out, cotangent):
    scale = 1.0 / (math.sqrt(HD) * math.sqrt(total_seqs))
    hbm = pl.BlockSpec(memory_space=pl.ANY)
    dma = pltpu.SemaphoreType.DMA
    result = jax.ShapeDtypeStruct((S, R, HW), BF)
    return pl.pallas_call(
        functools.partial(kernel, scale),
        out_shape=(result, result),
        in_specs=[hbm] * 6,
        out_specs=(hbm, hbm),
        scratch_shapes=[
            pltpu.VMEM((S, R, D), BF),
            pltpu.VMEM((S, R, D), BF),
            pltpu.VMEM((D, 6 * HW), BF),
            pltpu.VMEM((D, 6 * HW), BF),
            pltpu.VMEM((D, D), BF),
            pltpu.VMEM((D, D), BF),
            pltpu.VMEM((4, 12, R, 512), BF),
            pltpu.VMEM((S, R, D), BF),
            pltpu.VMEM((S, R, D), BF),
            pltpu.VMEM((S, R, HW), F32),
            pltpu.VMEM((6 * R, R), F32),
            pltpu.VMEM((6 * R, R), BF),
            pltpu.VMEM((6 * R, R), BF),
            pltpu.VMEM((6 * R, R), BF),
            pltpu.VMEM((3, 16, 2, 16, R), BF),
            pltpu.VMEM((15, 3, 2, 16, R), BF),
            pltpu.VMEM((3, 16, R), F32),
            pltpu.VMEM((3, 16, R), F32),
            pltpu.VMEM((3, 16, R), BF),
            pltpu.VMEM((2, 2, 3, 4, 4, 2, 16, R), BF),
            pltpu.VMEM((S, R, HW), BF),
            pltpu.VMEM((S, R, HW), BF),
            dma((20,)),
            dma((2, 4)), dma((2, 4)), dma((4,)), dma((4,)),
            dma((2,)), dma((2,)),
            dma, dma,
            dma, dma,
            dma, dma,
            dma((3,)), dma((3,)), dma((3, 4)), dma((3, 4)), dma((3, 4)), dma((3, 4)),
            dma((16,)),
        ],
        compiler_params=pltpu.CompilerParams(
            collective_id=0, has_side_effects=True, vmem_limit_bytes=62 * 2**20),
        cost_estimate=pl.CostEstimate(flops=18_500_000_000, bytes_accessed=15_000_000, transcendentals=12288),
        name="tied_row_attention",
    )(activations, w_query, w_key, w_value, w_out, cotangent)


def solution(mesh):
    total_seqs = S * mesh.shape["seq"]
    placed = (
        P("seq", None, None),
        P(None, "head"),
        P(None, "head"),
        P(None, "head"),
        P("head", None),
        P("seq", None, None),
    )
    return jax.shard_map(
        functools.partial(on_device, total_seqs),
        mesh=mesh,
        in_specs=placed,
        out_specs=(P("seq", None, "head"), P("seq", None, "head")),
        check_vma=False,
    )
```

```python
import functools
import math

import jax
import jax.numpy as jnp
from jax import lax
from jax.experimental import pallas as pl
from jax.experimental.pallas import tpu as pltpu
from jax.sharding import PartitionSpec as P

MESH = pl.DeviceIdType.MESH
BF, F32 = jnp.bfloat16, jnp.float32
S, R, D, HW, HD = 8, 256, 768, 384, 64
NT = (((1,), (1,)), ((), ()))
NN = (((1,), (0,)), ((), ()))
OWN = (0, 384, 768)
OTH = (1920, 1536, 1152)


def dot(a, b, dims=NN):
    return lax.dot_general(a, b, dims, preferred_element_type=F32)


def low_half(shape):
    return lax.broadcasted_iota(jnp.int32, shape, 1) < HD


def kernel(scale, act_hbm, wq_hbm, wk_hbm, wv_hbm, wo_hbm, cot_hbm, out_hbm, ig_hbm,
           act, cot, wn, ws, won, wos, xf, g2a, g2b, igp, keep, xs_l, xs_d, xr, rsend, rrecv, half_send, half_recv, pbuf, gat, outv, igv,
           load_sem, w_ss, w_rs, wc_ss, wc_rs, xc_ss, xc_rs, rs_ss, rs_rs, hc_ss, hc_rs, p_ss, p_rs,
           a1_ss, a1_rs, a2_ss, a2_rs, gc_ss, gc_rs, o_sem):
    seq, h = lax.axis_index("seq"), lax.axis_index("head")
    rem, div = lax.rem, lax.div
    c, xh, z, y = rem(seq, 2), rem(div(seq, 2), 2), rem(div(seq, 4), 4), div(seq, 16)
    ys, zs = [y], [z]
    for d in (1, 2, 3):
        ys.append(rem(y + d, 4))
        zs.append(rem(z + d, 4))
    x = xh * 2 + h
    xs_of = [(xh, h)]
    for d in (1, 2, 3):
        xx = rem(x + d, 4)
        xs_of.append((div(xx, 2), rem(xx, 2)))

    def dev(dy, dz, dx, cc=c):
        return ys[dy] * 16 + zs[dz] * 4 + xs_of[dx][0] * 2 + cc, xs_of[dx][1]

    sibling = dev(0, 0, 0, 1 - c)

    def remote(src, dst, ss, rs, to):
        return pltpu.make_async_remote_copy(
            src_ref=src, dst_ref=dst, send_sem=ss, recv_sem=rs, device_id=to, device_id_type=MESH)

    loads = [
        pltpu.make_async_copy(wq_hbm, wn.at[:, 0:384], load_sem.at[16]),
        pltpu.make_async_copy(wk_hbm, wn.at[:, 384:768], load_sem.at[17]),
        pltpu.make_async_copy(wv_hbm, wn.at[:, 768:1152], load_sem.at[18]),
        pltpu.make_async_copy(wo_hbm, won.at[0:384], load_sem.at[19]),
    ]

    def load_seq(hbm, buf, s, sem):
        return pltpu.make_async_copy(hbm.at[s], buf.at[s], load_sem.at[sem])

    loads[0].start()
    loads[1].start()
    for t in range(4):
        load_seq(act_hbm, act, t, t).start()
        load_seq(act_hbm, act, t + 4, t + 4).start()
    loads[2].start()
    loads[3].start()
    for s in range(S):
        load_seq(cot_hbm, cot, s, 8 + s).start()

    bar = pltpu.get_barrier_semaphore()

    def greet(to):
        pl.semaphore_signal(bar, inc=1, device_id=to, device_id_type=MESH)

    greet(sibling)
    for dy in range(4):
        for dz in range(4):
            for dx in range(4):
                if (dy, dz, dx) != (0, 0, 0) and (dx % 2 == 0 or dy == 0 or dz == 0):
                    greet(dev(dy, dz, dx))

    pl.semaphore_wait(bar, 46)

    def weight_copies():
        out = []
        for way, to in ((0, dev(0, 0, 1)), (1, dev(0, 0, 3))):
            rows = pl.ds(pl.multiple_of((2 * c + way) * 192, 192), 192)
            for i, src in enumerate((wq_hbm, wk_hbm, wv_hbm)):
                out.append(remote(src.at[rows], wn.at[rows, OTH[i]:OTH[i] + 384], w_ss.at[way, i], w_rs.at[way, i], to))
            rows = pl.ds(pl.multiple_of((2 * c + way) * 96, 96), 96)
            dst = pl.ds(pl.multiple_of(384 + (2 * c + way) * 96, 96), 96)
            out.append(remote(wo_hbm.at[rows], won.at[dst], w_ss.at[way, 3], w_rs.at[way, 3], to))
        return out

    def weight_forwards():
        out = []
        rows = pl.ds(pl.multiple_of(c * 384, 384), 384)
        for i in range(3):
            ref = wn.at[rows, OTH[i]:OTH[i] + 384]
            out.append(remote(ref, ref, wc_ss.at[i], wc_rs.at[i], sibling))
        ref = won.at[pl.ds(pl.multiple_of(384 + c * 192, 192), 192)]
        out.append(remote(ref, ref, wc_ss.at[3], wc_rs.at[3], sibling))
        return out

    for copy in weight_copies():
        copy.start()

    def swap_lanes(first, count):
        def rows(r, _):
            at = pl.ds(r * 128, 128)
            for j in range(first, first + count):
                block = wn[at, 128 * j:128 * j + 128]
                ws[at, 128 * j:128 * j + 128] = jnp.concatenate([block[:, HD:], block[:, :HD]], axis=1)
            return 0
        lax.fori_loop(0, 6, rows, 0, unroll=True)

    def swap_rows(base):
        for g in range(3):
            at = base + 128 * g
            wos[at:at + 64, :] = won[at + 64:at + 128, :]
            wos[at + 64:at + 128, :] = won[at:at + 64, :]

    def put(kind, head, t, even, odd):
        low = low_half(even.shape)
        lanes = pl.ds(pl.multiple_of(t * 128, 128), 128)
        xf[kind, head, :, lanes] = jnp.where(low, even, odd)
        xf[kind, head + 1, :, lanes] = jnp.where(low, odd, even)

    def project(t, lanes, places):
        even = dot(act[t], wn[:, lanes[0]:lanes[1]]).astype(BF)
        odd = dot(act[t + 4], ws[:, lanes[0]:lanes[1]]).astype(BF)
        for j, (kind, head) in enumerate(places):
            put(kind, head, t, even[:, 128 * j:128 * j + 128], odd[:, 128 * j:128 * j + 128])

    def project_ga(t, half):
        even = dot(cot[t], won[384 * half:384 * half + 384, :], NT).astype(BF)
        odd = dot(cot[t + 4], wos[384 * half:384 * half + 384, :], NT).astype(BF)
        for g in range(3):
            put(3, 6 * half + 2 * g, t, even[:, 128 * g:128 * g + 128], odd[:, 128 * g:128 * g + 128])

    loads[0].wait()
    loads[1].wait()
    swap_lanes(0, 6)

    def own_qk(t, _):
        load_seq(act_hbm, act, t, t).wait()
        load_seq(act_hbm, act, t + 4, t + 4).wait()
        project(t, (0, 768), [(0, 0), (0, 2), (0, 4), (1, 0), (1, 2), (1, 4)])
        return 0

    lax.fori_loop(0, 4, own_qk, 0, unroll=True)

    def pair_sum(left, right, mine, other, first):
        def head(i, _):
            total = dot(xf[left, i], xf[right, i], NT)
            at = pl.ds(pl.multiple_of(i * 256, 256), 256)
            mine[at, :] = total
            other[at, :] = total.astype(BF)
            return 0
        lax.fori_loop(first, first + 3, head, 0, unroll=True)

    def core_copy(src, part):
        at = pl.ds(part * 768, 768)
        return remote(src.at[at], xr.at[at], xc_ss.at[part], xc_rs.at[part], sibling)

    for part in (0, 1):
        pair_sum(0, 1, keep, xs_l, 3 * part)

        @pl.when(c == 1)
        def _():
            core_copy(xs_l, part).start()

    loads[2].wait()
    swap_lanes(6, 3)
    loads[3].wait()
    swap_rows(0)

    def own_v(t, _):
        project(t, (768, 1152), [(2, 0), (2, 2), (2, 4)])
        return 0


    me = y * 4 + z

    others = [(dy, dz) for dy in range(4) for dz in range(4)][1:]

    def rs_copy(i, dy, dz):
        return remote(rsend.at[:, ys[dy] * 4 + zs[dz]], rrecv.at[i], rs_ss, rs_rs, dev(dy, dz, 0))

    rs_all = remote(rrecv, rrecv, rs_ss, rs_rs, sibling)
    half_copy = remote(half_send, half_recv, hc_ss, hc_rs, dev(0, 0, 2))

    def send_sums():
        for part in (0, 1):
            core_copy(xs_l, part).wait_recv()

            def add(i, _):
                at = pl.ds(pl.multiple_of(i * 256, 256), 256)
                total = (keep[at, :] + xr[at, :].astype(F32)).astype(BF)
                rsend[i // 2, pl.ds((i % 2) * 8, 8)] = total.reshape(8, 2, 16, 256)
                return 0

            lax.fori_loop(3 * part, 3 * part + 3, add, 0, unroll=True)
        for i, where in enumerate(others):
            rs_copy(i, *where).start()

    def take_half(half):
        def add(d, total):
            return total + rrecv[d, :, half].astype(F32)

        return lax.fori_loop(0, 15, add, rsend[:, me, half].astype(F32), unroll=True)

    def take_sums():
        rs_all.wait_recv()
        half_send[...] = take_half(1 - xh)
        half_copy.start()
        own = take_half(xh)
        half_copy.wait_recv()
        return own + half_recv[...]

    def a1_copy(k, u, v):
        ref = gat.at[c, h, k, y, z, xh]
        to = (dev(u, v, 0), dev(0, u, v), dev(u, 0, v))[k]
        return remote(ref, ref, a1_ss.at[k], a1_rs.at[k], to)

    a1_all = [remote(rrecv.at[0:5, :, 0], rrecv.at[0:5, :, 0], a1_ss.at[k], a1_rs.at[k], sibling) for k in range(3)]

    def gather_own(block):
        for k in range(3):
            gat[c, h, k, y, z, xh] = block[k]
        for u in range(4):
            for v in range(4):
                if (u, v) != (0, 0):
                    for k in range(3):
                        a1_copy(k, u, v).start()

    def plane(k, d, part):
        if k == 0:
            return gat.at[c, xs_of[d][1], 0, 2 * part:2 * part + 2, :, xs_of[d][0]]
        if k == 1:
            return gat.at[c, part, 1, ys[d]]
        return gat.at[c, part, 2, :, zs[d]]

    def a2_copy(k, d, part):
        ref = plane(k, 0, part)
        to = (dev(0, 0, d), dev(d, 0, 0), dev(0, d, 0))[k]
        return remote(ref, ref, a2_ss.at[k, d, part], a2_rs.at[k, d, part], to)

    def forward(k, d, part):
        ref = plane(k, (4 - d) % 4, part)
        return remote(ref, ref, gc_ss.at[k, d, part], gc_rs.at[k, d, part], sibling)

    def gather_planes():
        for k in range(3):
            a1_all[k].wait_recv()
            for part in (0, 1):
                for d in (2, 1, 3):
                    a2_copy(k, d, part).start()
        for k in range(3):
            for part in (0, 1):
                forward(k, 0, part).start()

    def gather_rest(part):
        for d in (1, 3, 2):
            for k in (1, 2, 0):
                a2_copy(k, d, part).wait_recv()
                forward(k, d, part).start()

    def gather_other():
        for k in range(3):
            for d in range(4):
                for part in (0, 1):
                    forward(k, d, part).wait_recv()

    p_copy = remote(pbuf, pbuf, p_ss, p_rs, sibling)

    def softmax_step():
        logits = take_sums() * scale
        top = jnp.max(logits, axis=-1, keepdims=True)
        expd = jnp.exp(logits - top)
        probs = (expd / jnp.sum(expd, axis=-1, keepdims=True)).astype(BF)
        pbuf[...] = probs
        p_copy.start()
        gather_own(probs)

    def grad_step():
        dprob = take_sums()
        p_copy.wait_recv()
        probs = pbuf[...].astype(F32)
        inner = jnp.sum(probs * dprob, axis=-1, keepdims=True)
        gather_own((probs * (dprob - inner) * scale).astype(BF))

    def on_core(core, step):
        pl.when(c == core)(step)


    lax.fori_loop(0, 2, own_v, 0, unroll=True)
    on_core(0, send_sums)
    lax.fori_loop(2, 4, own_v, 0, unroll=True)

    def own_ga(t, _):
        load_seq(cot_hbm, cot, t, 8 + t).wait()
        load_seq(cot_hbm, cot, t + 4, 12 + t).wait()
        project_ga(t, 0)
        return 0

    lax.fori_loop(0, 4, own_ga, 0, unroll=True)
    for part in (0, 1):
        pair_sum(3, 2, keep, xs_d, 3 * part)
        on_core(0, core_copy(xs_d, part).start)
    on_core(1, send_sums)

    def other_qkv(t, _):
        project(t, (1152, 2304),
                [(2, 6), (2, 8), (2, 10), (1, 6), (1, 8), (1, 10), (0, 6), (0, 8), (0, 10)])
        return 0

    def other_ga(t, _):
        project_ga(t, 1)
        return 0

    on_core(0, softmax_step)
    for copy in weight_copies():
        copy.wait_recv()
    for copy in weight_forwards():
        copy.start()
    on_core(1, grad_step)
    for copy in weight_forwards():
        copy.wait_recv()
    swap_lanes(9, 9)
    swap_rows(384)
    lax.fori_loop(0, 2, other_qkv, 0, unroll=True)
    on_core(0, gather_planes)
    lax.fori_loop(2, 4, other_qkv, 0, unroll=True)
    lax.fori_loop(0, 4, other_ga, 0, unroll=True)
    on_core(1, gather_planes)
    on_core(0, functools.partial(gather_rest, 0))
    on_core(0, functools.partial(gather_rest, 1))
    on_core(1, gather_other)

    def pair_of(arr, g):
        half = (h + g // 3) % 2
        block = gat[arr, half, g % 3].reshape(512, 256)
        return block[:256], block[256:]

    def unput(first, second, refs):
        first, second = first.astype(BF), second.astype(BF)
        low = low_half((256, 128))
        for t in range(4):
            one, two = first[:, 128 * t:128 * t + 128], second[:, 128 * t:128 * t + 128]
            ref, lanes = refs
            ref[t, :, lanes] = jnp.where(low, one, two)
            ref[t + 4, :, lanes] = jnp.where(low, two, one)

    def lanes_at(start):
        return pl.ds(pl.multiple_of(start, 128), 128)

    att, gv = act, cot

    def with_probs(g, _):
        p0, p1 = pair_of(0, g)
        at = lanes_at(128 * g)
        unput(dot(p0, xf[2, 2 * g]), dot(p1, xf[2, 2 * g + 1]), (att, at))
        unput(dot(p0.T, xf[3, 2 * g]), dot(p1.T, xf[3, 2 * g + 1]), (gv, at))
        return 0

    lax.fori_loop(0, 6, with_probs, 0, unroll=True)

    own_cols = pl.ds(pl.multiple_of(h * 384, 384), 384)

    def out_copy(s):
        return pltpu.make_async_copy(outv.at[s], out_hbm.at[s], o_sem.at[s])

    def ig_copy(s):
        return pltpu.make_async_copy(igv.at[s], ig_hbm.at[s], o_sem.at[8 + s])

    def from_probs(t, _):
        for s, w_o, w in ((t, won, wn), (t + 4, wos, ws)):
            outv[s] = dot(att[s], w_o[:, own_cols]).astype(BF)
            out_copy(s).start()
            igp[s] = dot(gv[s], w[own_cols, 768:1536], NT)
        return 0

    on_core(1, functools.partial(gather_rest, 0))
    lax.fori_loop(0, 2, from_probs, 0, unroll=True)
    on_core(1, functools.partial(gather_rest, 1))
    lax.fori_loop(2, 4, from_probs, 0, unroll=True)
    on_core(0, gather_other)

    def with_grads(ref, first, query_at, key_at):
        def pair(i, _):
            g = first + i
            l0, l1 = pair_of(1, g)
            unput(dot(l0, xf[1, 2 * g]), dot(l1, xf[1, 2 * g + 1]), (ref, lanes_at(query_at + 128 * i)))
            unput(dot(l0.T, xf[0, 2 * g]), dot(l1.T, xf[0, 2 * g + 1]), (ref, lanes_at(key_at + 128 * i)))
            return 0
        lax.fori_loop(0, 3, pair, 0, unroll=True)

    with_grads(g2a, 0, 0, 384)
    with_grads(g2b, 3, 384, 0)

    def from_grads(t, _):
        for s, w in ((t, wn), (t + 4, ws)):
            total = igp[s] + dot(g2a[s], w[own_cols, 0:768], NT) + dot(g2b[s], w[own_cols, 1536:2304], NT)
            igv[s] = total.astype(BF)
            ig_copy(s).start()
        return 0

    for copy in weight_copies() + weight_forwards():
        copy.wait_send()
    on_core(0, p_copy.wait_send)
    rs_all.wait_send()
    half_copy.wait_send()
    for k in range(3):
        a1_all[k].wait_send()
        for d in range(4):
            for part in (0, 1):
                if d:
                    a2_copy(k, d, part).wait_send()
                forward(k, d, part).wait_send()
    for part in (0, 1):
        core_copy(xs_l, part).wait_send()

    lax.fori_loop(0, 4, from_grads, 0, unroll=True)

    def out_left(s, _):
        out_copy(s).wait()
        ig_copy(s).wait()
        return 0

    lax.fori_loop(0, S, out_left, 0)


def on_device(total_seqs, activations, w_query, w_key, w_value, w_out, cotangent):
    scale = 1.0 / (math.sqrt(HD) * math.sqrt(total_seqs))
    hbm = pl.BlockSpec(memory_space=pl.ANY)
    dma = pltpu.SemaphoreType.DMA
    result = jax.ShapeDtypeStruct((S, R, HW), BF)
    return pl.pallas_call(
        functools.partial(kernel, scale),
        out_shape=(result, result),
        in_specs=[hbm] * 6,
        out_specs=(hbm, hbm),
        scratch_shapes=[
            pltpu.VMEM((S, R, D), BF),
            pltpu.VMEM((S, R, D), BF),
            pltpu.VMEM((D, 6 * HW), BF),
            pltpu.VMEM((D, 6 * HW), BF),
            pltpu.VMEM((D, D), BF),
            pltpu.VMEM((D, D), BF),
            pltpu.VMEM((4, 12, R, 512), BF),
            pltpu.VMEM((S, R, D), BF),
            pltpu.VMEM((S, R, D), BF),
            pltpu.VMEM((S, R, HW), F32),
            pltpu.VMEM((6 * R, R), F32),
            pltpu.VMEM((6 * R, R), BF),
            pltpu.VMEM((6 * R, R), BF),
            pltpu.VMEM((6 * R, R), BF),
            pltpu.VMEM((3, 16, 2, 16, R), BF),
            pltpu.VMEM((15, 3, 2, 16, R), BF),
            pltpu.VMEM((3, 16, R), F32),
            pltpu.VMEM((3, 16, R), F32),
            pltpu.VMEM((3, 16, R), BF),
            pltpu.VMEM((2, 2, 3, 4, 4, 2, 16, R), BF),
            pltpu.VMEM((S, R, HW), BF),
            pltpu.VMEM((S, R, HW), BF),
            dma((20,)),
            dma((2, 4)), dma((2, 4)), dma((4,)), dma((4,)),
            dma((2,)), dma((2,)),
            dma, dma,
            dma, dma,
            dma, dma,
            dma((3,)), dma((3,)), dma((3, 4, 2)), dma((3, 4, 2)), dma((3, 4, 2)), dma((3, 4, 2)),
            dma((16,)),
        ],
        compiler_params=pltpu.CompilerParams(
            collective_id=0, has_side_effects=True, vmem_limit_bytes=62 * 2**20),
        cost_estimate=pl.CostEstimate(flops=18_500_000_000, bytes_accessed=15_000_000, transcendentals=12288),
        name="tied_row_attention",
    )(activations, w_query, w_key, w_value, w_out, cotangent)


def solution(mesh):
    total_seqs = S * mesh.shape["seq"]
    placed = (
        P("seq", None, None),
        P(None, "head"),
        P(None, "head"),
        P(None, "head"),
        P("head", None),
        P("seq", None, None),
    )
    return jax.shard_map(
        functools.partial(on_device, total_seqs),
        mesh=mesh,
        in_specs=placed,
        out_specs=(P("seq", None, "head"), P("seq", None, "head")),
        check_vma=False,
    )
```
